32 devices in a mesh: fsdp: 8 (over z, y), ctx: 4 (over x, core).
Axes of the slice: x: 2, y: 2, z: 4, core: 2. Of those that a mesh axis runs over, the one named last changes fastest.
Arguments:
- tokens: bfloat16 [2, 8, 256, 512], P(None, 'fsdp', 'ctx'), may hold values from -6 to 6
- cotangent: bfloat16 [2, 8, 256, 512], P(None, 'fsdp', 'ctx'), may hold values from -6 to 6
- doc_lengths: int32 [2, 8, 5], P(None, 'fsdp'), may hold values from 0 to 256, as said below
- w_qkv: bfloat16 [2, 512, 1536], P(None, ('fsdp', 'ctx')), may hold values from -0.25 to 0.25
- w_out: bfloat16 [2, 512, 512], P(None, ('fsdp', 'ctx')), may hold values from -1 to 1
- w_up: bfloat16 [2, 512, 2048], P(None, ('fsdp', 'ctx')), may hold values from -0.25 to 0.25
- w_down: bfloat16 [2, 2048, 512], P(None, ('fsdp', 'ctx')), may hold values from -0.125 to 0.125
- norm_gain: bfloat16 [2, 2, 512], P(None, None, ('fsdp', 'ctx')), may hold values from 0.25 to 1.75
- norm_bias: bfloat16 [2, 2, 512], P(None, None, ('fsdp', 'ctx')), may hold values from -1 to 1
- proj_bias: bfloat16 [2, 4608], P(None, ('fsdp', 'ctx')), may hold values from -1 to 1
Outputs:
- block_out: bfloat16 [2, 8, 256, 512], P(None, 'fsdp', 'ctx')
- grad_tokens: float32 [2, 8, 256, 512], P(None, 'fsdp', 'ctx')
- grad_w_qkv: float32 [2, 512, 1536], P(None, ('fsdp', 'ctx'))
- grad_w_out: float32 [2, 512, 512], P(None, ('fsdp', 'ctx'))
- grad_w_up: float32 [2, 512, 2048], P(None, ('fsdp', 'ctx'))
- grad_w_down: float32 [2, 2048, 512], P(None, ('fsdp', 'ctx'))
- grad_norm_gain: float32 [2, 2, 512], P(None, None, ('fsdp', 'ctx'))
- grad_norm_bias: float32 [2, 2, 512], P(None, None, ('fsdp', 'ctx'))
- grad_proj_bias: float32 [2, 4608], P(None, ('fsdp', 'ctx'))
The draws below stay inside these ranges and needn't reach their ends.
Inputs may be any that keep to these rules, and one draw needn't show every extreme that they name: `doc_lengths`: each pack's 5 document lengths sum to 256; zero lengths occur. In micro-batch 0 the third document of every pack starts within its first 64 positions and ends within its last 64, and in one pack of micro-batch 0 it fills all 256 positions.
All inputs are finite; a program needn't handle non-finite values.
Results may differ from the reference program's by a relative error of at most 0.015.
Values may be sent and summed in bfloat16 or wider, within the bound.
A program may use at most 192 MiB of HBM per device.

```python
import jax
import jax.numpy as jnp
from jax import lax

D = 512
HEAD = 64
FF = 2048
LAYERS = 2
MICRO = 2
DOCS = 5
PACK_DEV = 64
PACK = 256
PACKS = 8
BIAS = 4608


def draw_doc_lengths(key, part):
    key = jax.random.fold_in(key, 11)
    head_key, tail_key, whole_key, head_cut_key, tail_cut_key, cut_key = jax.random.split(key, 6)
    head_room = jax.random.randint(head_key, (PACKS,), 0, PACK_DEV)
    tail_room = jax.random.randint(tail_key, (PACKS,), 0, PACK_DEV)
    whole_index = jax.random.randint(whole_key, (), 0, PACKS)
    whole_pack = jnp.arange(PACKS, dtype=jnp.int32) == whole_index
    head_room = jnp.where(whole_pack, 0, head_room)
    tail_room = jnp.where(whole_pack, 0, tail_room)
    head_split = jax.random.randint(head_cut_key, (PACKS,), 0, head_room + 1)
    tail_split = jax.random.randint(tail_cut_key, (PACKS,), 0, tail_room + 1)
    spanning = PACK - head_room - tail_room
    leading = jnp.stack([head_split, head_room - head_split, spanning, tail_split, tail_room - tail_split], axis=1)
    cut_points = jnp.sort(jax.random.randint(cut_key, (MICRO - 1, PACKS, DOCS - 1), 0, PACK + 1), axis=-1)
    boundaries = jnp.concatenate([jnp.zeros((MICRO - 1, PACKS, 1), jnp.int32), cut_points, jnp.full((MICRO - 1, PACKS, 1), PACK, jnp.int32)], axis=-1)
    remaining = boundaries[..., 1:] - boundaries[..., :-1]
    return jnp.concatenate([leading[None], remaining], axis=0).astype(jnp.int32)


def shard_levels(rng, shape, shards, least, top_value):
    level, own = 1.0, jax.random.fold_in(rng, 6)
    for dim, shards_of in shards:
        steps = jnp.exp(jax.random.uniform(jax.random.fold_in(own, dim), (shards_of,), jnp.float32, least / len(shards), top_value / len(shards)))
        level = level * jnp.repeat(steps, shape[dim] // shards_of).reshape([-1 if axis == dim else 1 for axis in range(len(shape))])
    return level


def normal_values(own_key, shape, deviation, limit, pieces=(), held_as=jnp.bfloat16):
    values = jax.random.normal(own_key, shape, jnp.float32) * deviation
    if len(pieces) > 0:
        values = shard_levels(own_key, shape, pieces, -0.22, 0.18) * values
    return jnp.clip(values, min=-limit, max=limit).astype(held_as)


def setup_inputs(seed: int = 0) -> dict:
    key_of = jax.random.split(jax.random.key(seed), 11)
    tokens = normal_values(key_of[0], (MICRO, PACKS, PACK, D), 1.0, 6.0, ((1, 8), (2, 4)))
    cotangent = normal_values(key_of[1], (MICRO, PACKS, PACK, D), 1.0, 6.0, ((1, 8), (2, 4)))
    doc_lengths = draw_doc_lengths(jax.random.fold_in(key_of[10], 71), 0)
    w_qkv = normal_values(key_of[3], (LAYERS, D, 3 * D), D ** -0.5, 0.25, ((1, 32),))
    w_out = normal_values(key_of[4], (LAYERS, D, D), (D // 16) ** -0.5, 1.0, ((1, 32),))
    w_up = normal_values(key_of[5], (LAYERS, D, FF), D ** -0.5, 0.25, ((1, 32),))
    w_down = normal_values(key_of[6], (LAYERS, FF, D), FF ** -0.5, 0.125, ((1, 32),))
    norm_gain = jnp.clip(1.0 + 0.15 * jax.random.normal(key_of[7], (LAYERS, 2, D), jnp.float32), 0.25, 1.75).astype(jnp.bfloat16)
    norm_bias = normal_values(key_of[8], (LAYERS, 2, D), 0.2, 1.0, ((2, 32),))
    proj_bias = normal_values(key_of[9], (LAYERS, BIAS), 0.2, 1.0, ((1, 32),))
    return {"tokens": tokens, "cotangent": cotangent, "doc_lengths": doc_lengths, "w_qkv": w_qkv, "w_out": w_out, "w_up": w_up, "w_down": w_down, "norm_gain": norm_gain, "norm_bias": norm_bias, "proj_bias": proj_bias}


@jax.custom_vjp
def low(v):
    return lax.optimization_barrier(v.astype(jnp.bfloat16)).astype(jnp.float32)

@jax.custom_vjp
def low_back(v):
    return v

def low_keep(v):
    return (low(v), None)

def low_pass(kept, grad):
    return (grad,)

def back_keep(v):
    return (v, None)

def back_low(kept, grad):
    return (low(grad),)
low.defvjp(low_keep, low_pass)
low_back.defvjp(back_keep, back_low)
masked_score = -1e+30
norm_eps = 1e-05

def product(left, right):
    return jnp.dot(left, right, preferred_element_type=jnp.float32, precision=lax.Precision.HIGHEST)

def layer_norm(values, gain, shift):
    centred = values - lax.optimization_barrier(jnp.mean(values, axis=-1, keepdims=True))
    spread = lax.optimization_barrier(jnp.mean(centred * centred, axis=-1, keepdims=True))
    return centred * lax.rsqrt(spread + norm_eps) * gain + shift

def rotary_tables(positions):
    frequency = 10000.0 ** (-jnp.arange(8, dtype=jnp.float32) / 8.0)
    angles = positions.astype(jnp.float32)[:, None] * frequency[None, :]
    angles = jnp.concatenate([angles, angles], axis=1)
    return (jnp.cos(angles)[:, None, :], jnp.sin(angles)[:, None, :])

def rotate(heads_in, cos_table, sin_table):
    turned = heads_in[..., :16]
    swapped = jnp.concatenate([-turned[..., 8:], turned[..., :8]], axis=-1)
    return jnp.concatenate([turned * cos_table + swapped * sin_table, heads_in[..., 16:]], axis=-1)

def segments_of(lengths, positions):
    endings = jnp.cumsum(lengths).astype(jnp.int32)
    return lax.optimization_barrier(jnp.sum((endings[None, :] <= positions[:, None]).astype(jnp.int32), axis=1)).astype(jnp.int32)

def block_layer(values, weights, visible, cos_table, sin_table):
    w_qkv, w_out, w_up, w_down, gain_pair, shift_pair, biases = weights
    row_count, model_width = values.shape
    head_count = model_width // HEAD
    score_scale = HEAD ** (-0.5)
    normed = low(layer_norm(values, gain_pair[0], shift_pair[0]))
    mixed_qkv = low_back(product(normed, w_qkv) + biases[:3 * model_width])
    query_heads = low(rotate(mixed_qkv[:, :model_width].reshape(row_count, head_count, HEAD), cos_table, sin_table))
    key_heads = low(rotate(mixed_qkv[:, model_width:2 * model_width].reshape(row_count, head_count, HEAD), cos_table, sin_table))
    value_heads = low(mixed_qkv[:, 2 * model_width:].reshape(row_count, head_count, HEAD))
    scores = jnp.einsum('qhd,khd->hqk', query_heads, key_heads, precision=lax.Precision.HIGHEST) * score_scale
    scores = jnp.where(visible[None], low_back(scores), masked_score)
    soft_weights = jax.nn.softmax(scores, axis=-1)
    attended = jnp.einsum('hqk,khd->qhd', low(soft_weights), value_heads, precision=lax.Precision.HIGHEST)
    attended = low(low_back(attended.reshape(row_count, model_width)))
    branch_attn = low_back(product(attended, w_out) + biases[3 * model_width:4 * model_width])
    normed_mlp = low(layer_norm(values, gain_pair[1], shift_pair[1]))
    upward = low_back(product(normed_mlp, w_up) + biases[5 * model_width:])
    activated = low(jax.nn.gelu(upward, approximate=False))
    branch_mlp = low_back(product(activated, w_down) + biases[4 * model_width:5 * model_width])
    return values + branch_attn + branch_mlp

def reference(tokens, cotangent, doc_lengths, w_qkv, w_out, w_up, w_down, norm_gain, norm_bias, proj_bias):
    params = tuple((tensor.astype(jnp.float32) for tensor in (w_qkv, w_out, w_up, w_down, norm_gain, norm_bias, proj_bias)))
    micro_count, pack_count, pack_len, model_width = tokens.shape
    positions = jnp.arange(pack_len, dtype=jnp.int32)
    cos_table, sin_table = rotary_tables(positions)

    def one_pack(totals, sample):
        pack_tokens, pack_cot, lengths = sample
        segment = segments_of(lengths, positions)
        visible = (positions[None, :] <= positions[:, None]) & (segment[None, :] == segment[:, None])

        def stack_layers(values, layer_params):
            for layer_index in range(LAYERS):
                values = block_layer(values, tuple((stacked[layer_index] for stacked in layer_params)), visible, cos_table, sin_table)
            return values
        result, pullback = jax.vjp(stack_layers, pack_tokens.astype(jnp.float32), params)
        grad_input, grad_params = pullback(pack_cot.astype(jnp.float32))
        totals = tuple((running + gradient for running, gradient in zip(totals, grad_params)))
        return (totals, (result.astype(jnp.bfloat16), grad_input))
    starting = tuple((jnp.zeros(tensor.shape, jnp.float32) for tensor in params))
    packed = (tokens.reshape(micro_count * pack_count, pack_len, model_width), cotangent.reshape(micro_count * pack_count, pack_len, model_width), doc_lengths.reshape(micro_count * pack_count, -1))
    totals, (outputs, input_grads) = lax.scan(one_pack, starting, packed)
    return (outputs.reshape(tokens.shape), input_grads.reshape(tokens.shape), totals[0], totals[1], totals[2], totals[3], totals[4], totals[5], totals[6])
```

```python
import jax
import jax.numpy as jnp
from jax import lax
from jax.sharding import PartitionSpec as P

HEAD = 64
LANES = 128

masked_score = -1e30
norm_eps = 1e-05
low = jnp.bfloat16
wide = jnp.float32


def matmul(left, right):
    return jnp.dot(left, right, preferred_element_type=wide)


def matmul_tn(left, right):
    return lax.dot_general(left, right, (((0,), (0,)), ((), ())), preferred_element_type=wide)


def matmul_nt(left, right):
    return lax.dot_general(left, right, (((1,), (1,)), ((), ())), preferred_element_type=wide)


def normalise(values):
    centred = values - jnp.mean(values, axis=-1, keepdims=True)
    inverse = lax.rsqrt(jnp.mean(centred * centred, axis=-1, keepdims=True) + norm_eps)
    return centred * inverse, inverse


def rotary_tables(positions):
    frequency = 10000.0 ** (-jnp.arange(8, dtype=wide) / 8.0)
    angles = positions.astype(wide)[:, None] * frequency[None, :]
    angles = jnp.concatenate([angles, angles], axis=1)
    return jnp.cos(angles)[:, None, :], jnp.sin(angles)[:, None, :]


def rotate(heads_in, cos_table, sin_table):
    turned = heads_in[..., :16]
    swapped = jnp.concatenate([-turned[..., 8:], turned[..., :8]], axis=-1)
    return jnp.concatenate([turned * cos_table + swapped * sin_table, heads_in[..., 16:]], axis=-1)


def segments_of(lengths, positions):
    endings = jnp.cumsum(lengths, axis=-1)
    return jnp.sum((endings[:, None, :] <= positions[None, :, None]).astype(jnp.int32), axis=-1)


def slabs(array):
    pieces = array.shape[-1] // LANES
    return [array[..., LANES * i : LANES * (i + 1)] for i in range(pieces)]


def body(
    tokens, cotangent, doc_lengths, w_qkv, w_out, w_up, w_down, norm_gain, norm_bias, proj_bias
):
    micros, _, rows, width = tokens.shape
    layers = w_qkv.shape[0]
    C = lax.axis_size("ctx")
    F = lax.axis_size("fsdp")
    place = lax.axis_index("ctx")
    hidden = w_down.shape[1]
    depth = w_qkv.shape[1]
    local_qk = width // C
    heads = local_qk // HEAD
    local_ff = F * hidden
    pack_len = rows * C
    total_rows = C * micros * rows
    score_scale = HEAD ** (-0.5)
    own_bias = proj_bias.shape[1]
    own_small = own_bias + 4 * depth
    small_pad = -(-own_small // LANES) * LANES
    out_rows = local_qk // F

    forth = [(b, (b % F) * C + b // F) for b in range(F * C)]
    back = [(there, here) for here, there in forth]

    small_own = jnp.concatenate(
        [proj_bias, norm_gain.reshape(layers, -1), norm_bias.reshape(layers, -1)], axis=1
    )
    small_own = jnp.pad(small_own, ((0, 0), (0, small_pad - own_small)))
    qkv_cols = w_qkv.reshape(layers, depth, 3, C, local_qk).transpose(3, 0, 2, 1, 4)
    up_cols = w_up.reshape(layers, depth, F, C, hidden).transpose(3, 0, 1, 2, 4)
    up_cols = up_cols.reshape(C, layers, depth, local_ff // LANES, LANES).transpose(0, 1, 3, 2, 4)
    spread = jnp.concatenate(
        [
            qkv_cols.reshape(C, layers, -1, LANES),
            up_cols.reshape(C, layers, -1, LANES),
            jnp.broadcast_to(
                small_own.reshape(1, layers, -1, LANES), (C, layers, small_pad // LANES, LANES)
            ),
        ],
        axis=2,
    )
    arrived = lax.all_to_all(spread, "ctx", 0, 0, tiled=False)
    w_out_here = lax.ppermute(w_out, ("fsdp", "ctx"), forth)
    n_qkv = 3 * depth
    n_up = local_ff // LANES * depth
    column_slabs = 3 + local_ff // LANES

    tokens_rows = tokens.reshape(micros * rows, width)
    cot_rows = cotangent.reshape(micros * rows, width)
    both = lax.all_gather(jnp.stack([tokens_rows, cot_rows]), "ctx", axis=0)
    values_all = both[:, 0].reshape(total_rows, width).astype(wide)
    cot_all = both[:, 1].reshape(total_rows, width)

    def layer_weights(layer):
        part = arrived[:, layer]
        down_slabs = jnp.concatenate(slabs(w_down[layer]), axis=0)
        out_slabs = jnp.concatenate(slabs(w_out_here[layer]), axis=0)
        payload = jnp.concatenate(
            [part.reshape(-1, LANES), down_slabs, out_slabs], axis=0
        )
        size = payload.shape[0]
        if layer == 0:
            gathered = lax.all_to_all(
                jnp.broadcast_to(payload[None], (F, size, LANES)), "fsdp", 0, 0, tiled=False
            )
        else:
            gathered = lax.all_gather(payload, "fsdp", axis=0)
        n_part = part.size // LANES
        columns = gathered[:, :n_part].reshape(F, C, -1, LANES)
        qkv = columns[:, :, :n_qkv].reshape(F, C, 3, depth, LANES)
        qkv = [qkv[:, :, i].reshape(width, LANES) for i in range(3)]
        up = columns[:, :, n_qkv : n_qkv + n_up].reshape(F, C, -1, depth, LANES)
        up = [up[:, :, i].reshape(width, LANES) for i in range(local_ff // LANES)]
        small = columns[:, :, n_qkv + n_up :].reshape(F, C, small_pad).astype(wide)
        down = gathered[:, n_part : n_part + down_slabs.shape[0]].reshape(F, -1, hidden, LANES)
        down = [down[:, i].reshape(local_ff, LANES) for i in range(width // LANES)]
        out = gathered[:, n_part + down_slabs.shape[0] :].reshape(F, -1, out_rows, LANES)
        out = [out[:, i].reshape(local_qk, LANES) for i in range(width // LANES)]
        biases = small[:, :, :own_bias].reshape(-1)
        gains = small[:, :, own_bias : own_bias + 2 * depth].reshape(F * C, 2, depth)
        gains = gains.transpose(1, 0, 2).reshape(2, width)
        shifts = small[:, :, own_bias + 2 * depth : own_small].reshape(F * C, 2, depth)
        shifts = shifts.transpose(1, 0, 2).reshape(2, width)
        b_qkv = biases[: 3 * width].reshape(3, C, local_qk)
        b_qkv = lax.dynamic_slice_in_dim(b_qkv, place, 1, 1).reshape(-1)
        b_up = biases[5 * width :].reshape(F, C, hidden)
        b_up = lax.dynamic_slice_in_dim(b_up, place, 1, 1).reshape(-1)
        b_rest = biases[3 * width : 4 * width] + biases[4 * width : 5 * width]
        return (
            jnp.concatenate(qkv, axis=1),
            jnp.concatenate(out, axis=1),
            jnp.concatenate(up, axis=1),
            jnp.concatenate(down, axis=1),
            gains,
            shifts,
            b_qkv,
            b_up,
            b_rest,
        )

    def sum_rows(partial):
        parts = partial.astype(low).reshape(C, micros * rows, width)
        parts = lax.all_to_all(parts, "ctx", 0, 0, tiled=False)
        return jnp.sum(parts.astype(wide), axis=0)

    def gather_rows(own):
        return lax.all_gather(own, "ctx", axis=0).reshape(total_rows, width)

    positions = jnp.arange(pack_len, dtype=jnp.int32)
    seg = segments_of(doc_lengths[:, 0], positions)
    visible = (positions[None, None, :] <= positions[None, :, None]) & (
        seg[:, None, :] == seg[:, :, None]
    )
    visible = visible[:, None]
    row_positions = jnp.broadcast_to(
        positions.reshape(C, 1, rows), (C, micros, rows)
    ).reshape(-1)
    cos_table, sin_table = rotary_tables(row_positions)

    def to_packs(array):
        array = array.reshape(C, micros, rows, heads, HEAD).transpose(1, 3, 0, 2, 4)
        return array.reshape(micros, heads, pack_len, HEAD)

    def from_packs(array):
        array = array.reshape(micros, heads, C, rows, HEAD).transpose(2, 0, 3, 1, 4)
        return array.reshape(total_rows, local_qk)

    def turn(array, sin_signed):
        return rotate(array.reshape(total_rows, heads, HEAD), cos_table, sin_signed)

    def batched(spec, left, right):
        return jnp.einsum(spec, left, right, preferred_element_type=wide)

    all_weights = [layer_weights(layer) for layer in range(layers)]

    kept_layers = []
    own_values = tokens_rows.astype(wide)
    for layer in range(layers):
        qkv, out, up, down, gains, shifts, b_qkv, b_up, b_rest = all_weights[layer]
        unit, _ = normalise(values_all)
        h1 = (unit * gains[0] + shifts[0]).astype(low)
        h2 = (unit * gains[1] + shifts[1]).astype(low)
        mixed = matmul(h1, qkv) + b_qkv
        query = to_packs(turn(mixed[:, :local_qk], sin_table).astype(low))
        key = to_packs(turn(mixed[:, local_qk : 2 * local_qk], sin_table).astype(low))
        value = to_packs(mixed[:, 2 * local_qk :].astype(low))
        scores = batched("mhqd,mhkd->mhqk", query, key) * score_scale
        scores = jnp.where(visible, scores, masked_score)
        peak = jnp.max(scores, axis=-1, keepdims=True)
        exps = jnp.exp(scores - peak)
        soft = exps / jnp.sum(exps, axis=-1, keepdims=True)
        soft_low = soft.astype(low)
        attended = from_packs(batched("mhqk,mhkd->mhqd", soft_low, value).astype(low))
        upward = matmul(h2, up) + b_up
        active = jax.nn.gelu(upward, approximate=False).astype(low)
        change = sum_rows(matmul(attended, out) + matmul(active, down)) + b_rest
        kept_layers.append(
            (values_all, own_values, h1, h2, query, key, value, soft, attended, upward, active)
        )
        own_values = own_values + change
        if layer + 1 < layers:
            values_all = gather_rows(own_values)
    block_out = own_values.astype(low).reshape(micros, 1, rows, width)

    own_grad = cot_rows.astype(wide)
    cot_low = cot_all
    mine = (jnp.arange(C) == place).astype(wide)
    pieces = [None] * layers
    for layer in reversed(range(layers)):
        qkv, out, up, down, gains, shifts, b_qkv, b_up, b_rest = all_weights[layer]
        values, own_in, h1, h2, query, key, value, soft, attended, upward, active = kept_layers[
            layer
        ]
        d_down = matmul_tn(active, cot_low)
        d_out = matmul_tn(attended, cot_low)
        db_rest = jnp.sum(own_grad.astype(low).astype(wide), axis=0)
        d_active = matmul_nt(cot_low, down)
        _, gelu_pull = jax.vjp(lambda u: jax.nn.gelu(u, approximate=False), upward)
        d_upward = gelu_pull(d_active)[0].astype(low)
        d_up = matmul_tn(h2, d_upward)
        db_up = jnp.sum(d_upward.astype(wide), axis=0)
        d_h2 = matmul_nt(d_upward, up)
        d_att = to_packs(matmul_nt(cot_low, out).astype(low))
        d_soft = batched("mhqd,mhkd->mhqk", d_att, value)
        d_value = batched("mhqk,mhqd->mhkd", soft.astype(low), d_att)
        inner = jnp.sum(soft * d_soft, axis=-1, keepdims=True)
        d_scores = (soft * (d_soft - inner)).astype(low)
        d_query = batched("mhqk,mhkd->mhqd", d_scores, key) * score_scale
        d_key = batched("mhqk,mhqd->mhkd", d_scores, query) * score_scale
        d_mixed = jnp.concatenate(
            [
                turn(from_packs(d_query), -sin_table).reshape(total_rows, local_qk),
                turn(from_packs(d_key), -sin_table).reshape(total_rows, local_qk),
                from_packs(d_value),
            ],
            axis=1,
        ).astype(low)
        d_qkv = matmul_tn(h1, d_mixed)
        db_qkv = jnp.sum(d_mixed.astype(wide), axis=0)
        d_h1 = matmul_nt(d_mixed, qkv)
        unit, _ = normalise(values)
        dg = jnp.stack([jnp.sum(d_h1 * unit, axis=0), jnp.sum(d_h2 * unit, axis=0)])
        ds = jnp.stack([jnp.sum(d_h1, axis=0), jnp.sum(d_h2, axis=0)])
        flow = sum_rows(d_h1 * gains[0] + d_h2 * gains[1])
        unit_own, inverse = normalise(own_in)
        flow = flow - jnp.mean(flow, axis=-1, keepdims=True) - unit_own * jnp.mean(
            flow * unit_own, axis=-1, keepdims=True
        )
        own_grad = own_grad + inverse * flow
        if layer > 0:
            cot_low = gather_rows(own_grad.astype(low))

        db_qkv = (db_qkv.reshape(3, 1, local_qk) * mine[None, :, None]).reshape(-1)
        db_up = (db_up.reshape(F, 1, hidden) * mine[None, :, None]).reshape(-1)
        db = jnp.concatenate([db_qkv, db_rest, db_rest, db_up]).reshape(F * C, own_bias)
        dg = dg.reshape(2, F * C, depth).transpose(1, 0, 2).reshape(F * C, 2 * depth)
        ds = ds.reshape(2, F * C, depth).transpose(1, 0, 2).reshape(F * C, 2 * depth)
        small = jnp.concatenate(
            [db, dg, ds, jnp.zeros((F * C, small_pad - own_small), wide)], axis=1
        )
        payload = jnp.concatenate(
            slabs(d_qkv.reshape(F, C * depth, 3 * local_qk).astype(low))
            + slabs(d_up.reshape(F, C * depth, local_ff).astype(low))
            + slabs(d_down.reshape(F, hidden, width).astype(low))
            + slabs(d_out.reshape(F, out_rows, width).astype(low))
            + [small.astype(low).reshape(F, -1, LANES)],
            axis=1,
        )
        parts = lax.all_to_all(payload, "fsdp", 0, 0, tiled=False)
        pieces[layer] = jnp.sum(parts.astype(wide), axis=0)
    grad_tokens = own_grad.reshape(micros, 1, rows, width)

    merged = jnp.stack(pieces)
    n_cols = column_slabs * C * depth
    n_down = width // LANES * hidden
    n_out = width // LANES * out_rows
    cols = merged[:, :n_cols].reshape(layers, column_slabs, C, depth, LANES)
    cols = cols.transpose(2, 0, 1, 3, 4).reshape(C, layers, -1, LANES)
    small = merged[:, n_cols + n_down + n_out :].reshape(layers, C, -1, LANES).transpose(1, 0, 2, 3)
    home = lax.all_to_all(jnp.concatenate([cols, small], axis=2), "ctx", 0, 0, tiled=False)
    down_sum = merged[:, n_cols : n_cols + n_down].reshape(layers, -1, hidden, LANES)
    grad_down = down_sum.transpose(0, 2, 1, 3).reshape(layers, hidden, width)
    out_sum = merged[:, n_cols + n_down : n_cols + n_down + n_out]
    out_sum = out_sum.reshape(layers, -1, out_rows, LANES).transpose(0, 2, 1, 3)
    grad_out = lax.ppermute(out_sum.reshape(layers, out_rows, width), ("fsdp", "ctx"), back)

    n_own = column_slabs * depth
    columns = home[:, :, :n_own].reshape(C, layers, column_slabs, depth, LANES)
    grad_qkv = columns[:, :, :3].transpose(1, 3, 2, 0, 4).reshape(layers, depth, 3 * width)
    grad_up = columns[:, :, 3:].transpose(0, 1, 3, 2, 4).reshape(C, layers, depth, F, hidden)
    grad_up = grad_up.transpose(1, 2, 3, 0, 4).reshape(layers, depth, F * C * hidden)
    small = jnp.sum(home[:, :, n_own:], axis=0).reshape(layers, small_pad)
    grad_bias = small[:, :own_bias]
    grad_gain = small[:, own_bias : own_bias + 2 * depth].reshape(layers, 2, depth)
    grad_shift = small[:, own_bias + 2 * depth : own_small].reshape(layers, 2, depth)
    return (
        block_out,
        grad_tokens,
        grad_qkv,
        grad_out,
        grad_up,
        grad_down,
        grad_gain,
        grad_shift,
        grad_bias,
    )


def solution(mesh):
    weight = P(None, ("fsdp", "ctx"), None)
    rows = P(None, "fsdp", "ctx", None)
    feature = P(None, None, ("fsdp", "ctx"))
    flat = P(None, ("fsdp", "ctx"))
    return jax.shard_map(
        body,
        mesh=mesh,
        in_specs=(
            rows,
            rows,
            P(None, "fsdp", None),
            weight,
            weight,
            weight,
            weight,
            feature,
            feature,
            flat,
        ),
        out_specs=(rows, rows, weight, weight, weight, weight, feature, feature, flat),
        check_vma=False,
    )
```

```python
import functools

import jax
import jax.numpy as jnp
from jax import lax
from jax.experimental import pallas as pl
from jax.experimental.pallas import tpu as pltpu
from jax.sharding import PartitionSpec as P

HEAD = 64
LANES = 128

masked_score = -1e30
norm_eps = 1e-05
low = jnp.bfloat16
wide = jnp.float32


def matmul(left, right):
    return jnp.dot(left, right, preferred_element_type=wide)


def matmul_tn(left, right):
    return lax.dot_general(left, right, (((0,), (0,)), ((), ())), preferred_element_type=wide)


def matmul_nt(left, right):
    return lax.dot_general(left, right, (((1,), (1,)), ((), ())), preferred_element_type=wide)


def normalise(values):
    centred = values - jnp.mean(values, axis=-1, keepdims=True)
    inverse = lax.rsqrt(jnp.mean(centred * centred, axis=-1, keepdims=True) + norm_eps)
    return centred * inverse, inverse


def rotary_tables(positions, columns):
    lane = jnp.arange(columns, dtype=jnp.int32) % HEAD
    frequency = 10000.0 ** (-(lane % 8).astype(wide) / 8.0)
    angles = positions.astype(wide)[:, None] * frequency[None, :]
    cos, sin = jnp.cos(angles), jnp.sin(angles)
    return jnp.stack(
        [
            jnp.where(lane < 16, cos, 1.0),
            jnp.where((lane >= 8) & (lane < 16), sin, 0.0),
            jnp.where(lane < 8, -sin, 0.0),
        ]
    )


def turned(array, own, before, after):
    return (
        array * own
        + pltpu.roll(array, 8, 1) * before
        + pltpu.roll(array, array.shape[1] - 8, 1) * after
    )


def pack_rows(array, micro, micros, places):
    rows = array.shape[0] // (micros * places)
    starts = [(place * micros + micro) * rows for place in range(places)]
    return jnp.concatenate([array[start : start + rows] for start in starts], axis=0)


def put_rows(ref, columns, array, micro, micros, places):
    rows = array.shape[0] // places
    for place in range(places):
        start = (place * micros + micro) * rows
        ref[start : start + rows, columns] = array[place * rows : (place + 1) * rows]


def phi_of(upward):
    return 0.5 * (1.0 + lax.erf(upward * (0.5**0.5)))


def forward_kernel(
    micros,
    places,
    x_ref,
    qkv_ref,
    out_ref,
    up_ref,
    down_ref,
    gain_ref,
    shift_ref,
    b_qkv_ref,
    b_up_ref,
    table_ref,
    visible_ref,
    change_ref,
    h1_ref,
    h2_ref,
    mixed_ref,
    soft_ref,
    att_ref,
    upward_ref,
    active_ref,
):
    local = out_ref.shape[0]
    heads = local // HEAD
    unit, _ = normalise(x_ref[...])
    h1_ref[...] = (unit * gain_ref[0:1] + shift_ref[0:1]).astype(low)
    h2_ref[...] = (unit * gain_ref[1:2] + shift_ref[1:2]).astype(low)
    mixed = matmul(h1_ref[...], qkv_ref[...]) + b_qkv_ref[...]
    tables = [table_ref[i] for i in range(3)]
    mixed_ref[:, :local] = turned(mixed[:, :local], *tables).astype(low)
    mixed_ref[:, local : 2 * local] = turned(mixed[:, local : 2 * local], *tables).astype(low)
    mixed_ref[:, 2 * local :] = mixed[:, 2 * local :].astype(low)
    lane = lax.broadcasted_iota(jnp.int32, (1, local), 1) // HEAD
    for micro in range(micros):
        whole = pack_rows(mixed_ref[...], micro, micros, places)
        query, key, value = (whole[:, i * local : (i + 1) * local] for i in range(3))
        seen = visible_ref[micro] > 0.5
        attended = jnp.zeros((whole.shape[0], local), wide)
        for head in range(heads):
            here = lane == head
            scores = matmul_nt(jnp.where(here, query, jnp.zeros_like(query)), key)
            scores = jnp.where(seen, scores * HEAD**-0.5, masked_score)
            exps = jnp.exp(scores - jnp.max(scores, axis=-1, keepdims=True))
            soft = exps / jnp.sum(exps, axis=-1, keepdims=True)
            soft_ref[micro * heads + head] = soft
            attended = jnp.where(here, matmul(soft.astype(low), value), attended)
        put_rows(att_ref, slice(0, local), attended.astype(low), micro, micros, places)
    upward = matmul(h2_ref[...], up_ref[...]) + b_up_ref[...]
    upward_ref[...] = upward
    active_ref[...] = (upward * phi_of(upward)).astype(low)
    change_ref[...] = (
        matmul(att_ref[...], out_ref[...]) + matmul(active_ref[...], down_ref[...])
    ).astype(low)


def backward_kernel(
    micros,
    places,
    cot_ref,
    x_ref,
    qkv_ref,
    out_ref,
    up_ref,
    down_ref,
    gain_ref,
    table_ref,
    h1_ref,
    h2_ref,
    mixed_ref,
    soft_ref,
    att_ref,
    upward_ref,
    active_ref,
    flow_ref,
    d_qkv_ref,
    d_out_ref,
    d_up_ref,
    d_down_ref,
    db_qkv_ref,
    db_up_ref,
    dg_ref,
    ds_ref,
    d_turned,
    d_mixed,
):
    local = out_ref.shape[0]
    heads = local // HEAD
    cot = cot_ref[...]
    d_att = matmul_nt(cot, out_ref[...]).astype(low)
    lane = lax.broadcasted_iota(jnp.int32, (1, local), 1) // HEAD
    for micro in range(micros):
        whole = pack_rows(mixed_ref[...], micro, micros, places)
        query, key, value = (whole[:, i * local : (i + 1) * local] for i in range(3))
        d_own = pack_rows(d_att, micro, micros, places)
        d_query = jnp.zeros(query.shape, wide)
        d_key, d_value = d_query, d_query
        for head in range(heads):
            here = lane == head
            soft = soft_ref[micro * heads + head]
            d_soft = matmul_nt(jnp.where(here, d_own, jnp.zeros_like(d_own)), value)
            d_value = jnp.where(here, matmul_tn(soft.astype(low), d_own), d_value)
            inner = jnp.sum(soft * d_soft, axis=-1, keepdims=True)
            d_scores = (soft * (d_soft - inner)).astype(low)
            d_query = jnp.where(here, matmul(d_scores, key), d_query)
            d_key = jnp.where(here, matmul_tn(d_scores, query), d_key)
        scale = HEAD**-0.5
        put_rows(d_turned, slice(0, local), d_query * scale, micro, micros, places)
        put_rows(d_turned, slice(local, 2 * local), d_key * scale, micro, micros, places)
        put_rows(d_turned, slice(2 * local, 3 * local), d_value, micro, micros, places)
    tables = (table_ref[0], -table_ref[1], -table_ref[2])
    d_mixed[:, :local] = turned(d_turned[:, :local], *tables).astype(low)
    d_mixed[:, local : 2 * local] = turned(d_turned[:, local : 2 * local], *tables).astype(low)
    d_mixed[:, 2 * local :] = d_turned[:, 2 * local :].astype(low)
    d_qkv_ref[...] = matmul_tn(h1_ref[...], d_mixed[...]).astype(low)
    db_qkv_ref[...] = jnp.sum(d_mixed[...].astype(wide), axis=0, keepdims=True)
    d_down_ref[...] = matmul_tn(active_ref[...], cot).astype(low)
    d_out_ref[...] = matmul_tn(att_ref[...], cot).astype(low)
    upward = upward_ref[...]
    slope = phi_of(upward) + upward * (jnp.exp(-0.5 * upward * upward) * 0.3989422804014327)
    d_upward = (matmul_nt(cot, down_ref[...]) * slope).astype(low)
    d_up_ref[...] = matmul_tn(h2_ref[...], d_upward).astype(low)
    db_up_ref[...] = jnp.sum(d_upward.astype(wide), axis=0, keepdims=True)
    unit, _ = normalise(x_ref[...])
    d_h1 = matmul_nt(d_mixed[...], qkv_ref[...])
    dg_ref[0:1] = jnp.sum(d_h1 * unit, axis=0, keepdims=True)
    ds_ref[0:1] = jnp.sum(d_h1, axis=0, keepdims=True)
    d_h2 = matmul_nt(d_upward, up_ref[...])
    dg_ref[1:2] = jnp.sum(d_h2 * unit, axis=0, keepdims=True)
    ds_ref[1:2] = jnp.sum(d_h2, axis=0, keepdims=True)
    flow_ref[...] = (d_h1 * gain_ref[0:1] + d_h2 * gain_ref[1:2]).astype(low)


def assemble_kernel(places, gathered_ref, qkv_ref, out_ref, up_ref, down_ref):
    shards = gathered_ref.shape[0]
    depth = qkv_ref.shape[0] // (shards * places)
    hidden, out_rows = down_ref.shape[0] // shards, out_ref.shape[0] // shards
    for shard in range(shards):
        start = 0
        for place in range(places):
            first = (shard * places + place) * depth
            for target in (qkv_ref, up_ref):
                for left in range(0, target.shape[1], LANES):
                    target[first : first + depth, left : left + LANES] = gathered_ref[
                        shard, start : start + depth
                    ]
                    start += depth
        for target, size in ((down_ref, hidden), (out_ref, out_rows)):
            for left in range(0, target.shape[1], LANES):
                target[shard * size : (shard + 1) * size, left : left + LANES] = gathered_ref[
                    shard, start : start + size
                ]
                start += size


def pack_kernel(qkv_ref, up_ref, down_ref, out_ref, small_ref, payload_ref):
    shards = payload_ref.shape[0]
    for shard in range(shards):
        start = 0
        for source in (qkv_ref, up_ref, down_ref, out_ref):
            size = source.shape[0] // shards
            for left in range(0, source.shape[1], LANES):
                payload_ref[shard, start : start + size] = source[
                    shard * size : (shard + 1) * size, left : left + LANES
                ]
                start += size
        payload_ref[shard, start : start + small_ref.shape[1]] = small_ref[shard]


def call(kernel, outs, scratch, *args):
    return pl.pallas_call(
        kernel,
        out_shape=[jax.ShapeDtypeStruct(shape, kind) for shape, kind in outs],
        in_specs=[pl.BlockSpec(memory_space=pltpu.VMEM)] * len(args),
        out_specs=[pl.BlockSpec(memory_space=pltpu.VMEM)] * len(outs),
        scratch_shapes=[pltpu.VMEM(shape, kind) for shape, kind in scratch],
        compiler_params=pltpu.CompilerParams(vmem_limit_bytes=40 * 1024 * 1024),
        cost_estimate=pl.CostEstimate(
            flops=3_000_000_000, bytes_accessed=10_000_000, transcendentals=1_000_000
        ),
    )(*args)


def segments_of(lengths, positions):
    endings = jnp.cumsum(lengths, axis=-1)
    return jnp.sum((endings[:, None, :] <= positions[None, :, None]).astype(jnp.int32), axis=-1)


def slabs(array):
    pieces = array.shape[-1] // LANES
    return [array[..., LANES * i : LANES * (i + 1)] for i in range(pieces)]


def body(
    tokens, cotangent, doc_lengths, w_qkv, w_out, w_up, w_down, norm_gain, norm_bias, proj_bias
):
    micros, _, rows, width = tokens.shape
    layers = w_qkv.shape[0]
    C = lax.axis_size("ctx")
    F = lax.axis_size("fsdp")
    place = lax.axis_index("ctx")
    hidden = w_down.shape[1]
    depth = w_qkv.shape[1]
    local_qk = width // C
    heads = local_qk // HEAD
    local_ff = F * hidden
    pack_len = rows * C
    total_rows = C * micros * rows
    score_scale = HEAD ** (-0.5)
    own_bias = proj_bias.shape[1]
    own_small = own_bias + 4 * depth
    small_pad = -(-own_small // LANES) * LANES
    out_rows = local_qk // F

    forth = [(b, (b % F) * C + b // F) for b in range(F * C)]
    back = [(there, here) for here, there in forth]

    small_own = jnp.concatenate(
        [proj_bias, norm_gain.reshape(layers, -1), norm_bias.reshape(layers, -1)], axis=1
    )
    small_own = jnp.pad(small_own, ((0, 0), (0, small_pad - own_small)))
    qkv_cols = w_qkv.reshape(layers, depth, 3, C, local_qk).transpose(3, 0, 2, 1, 4)
    up_cols = w_up.reshape(layers, depth, F, C, hidden).transpose(3, 0, 1, 2, 4)
    up_cols = up_cols.reshape(C, layers, depth, local_ff // LANES, LANES).transpose(0, 1, 3, 2, 4)
    spread = jnp.concatenate(
        [
            qkv_cols.reshape(C, layers, -1, LANES),
            up_cols.reshape(C, layers, -1, LANES),
            jnp.broadcast_to(
                small_own.reshape(1, layers, -1, LANES), (C, layers, small_pad // LANES, LANES)
            ),
        ],
        axis=2,
    )
    arrived = lax.all_to_all(spread, "ctx", 0, 0, tiled=False)
    w_out_here = lax.ppermute(w_out, ("fsdp", "ctx"), forth)
    aligned = depth % 16 == 0 and hidden % 16 == 0 and out_rows % 16 == 0
    n_qkv = 3 * depth
    n_up = local_ff // LANES * depth
    column_slabs = 3 + local_ff // LANES

    tokens_rows = tokens.reshape(micros * rows, width)
    cot_rows = cotangent.reshape(micros * rows, width)
    values_all = lax.all_gather(tokens_rows, "ctx", axis=0).reshape(total_rows, width)
    values_all = values_all.astype(wide)
    cot_all = lax.all_gather(cot_rows, "ctx", axis=0).reshape(total_rows, width)

    def gather_layer(layer):
        part = arrived[:, layer]
        payload = jnp.concatenate(
            [part[:, : n_qkv + n_up].reshape(-1, LANES)]
            + slabs(w_down[layer])
            + slabs(w_out_here[layer])
            + [part[:, n_qkv + n_up :].reshape(-1, LANES)],
            axis=0,
        )
        size = payload.shape[0]
        if layer == 0:
            return lax.all_to_all(
                jnp.broadcast_to(payload[None], (F, size, LANES)), "fsdp", 0, 0, tiled=False
            )
        return lax.all_gather(payload, "fsdp", axis=0)

    def layer_weights(gathered):
        n_small = C * small_pad // LANES
        n_part = C * (n_qkv + n_up)
        n_down = width // LANES * hidden
        if aligned:
            qkv, out, up, down = call(
                functools.partial(assemble_kernel, C),
                [
                    ((width, 3 * local_qk), low),
                    ((local_qk, width), low),
                    ((width, local_ff), low),
                    ((local_ff, width), low),
                ],
                [],
                gathered,
            )
        else:
            columns = gathered[:, :n_part].reshape(F, C, -1, LANES)
            qkv = columns[:, :, :n_qkv].reshape(F, C, 3, depth, LANES)
            qkv = jnp.concatenate([qkv[:, :, i].reshape(width, LANES) for i in range(3)], axis=1)
            up = columns[:, :, n_qkv:].reshape(F, C, -1, depth, LANES)
            up = [up[:, :, i].reshape(width, LANES) for i in range(local_ff // LANES)]
            up = jnp.concatenate(up, axis=1)
            down = gathered[:, n_part : n_part + n_down].reshape(F, -1, hidden, LANES)
            down = [down[:, i].reshape(local_ff, LANES) for i in range(width // LANES)]
            down = jnp.concatenate(down, axis=1)
            out = gathered[:, n_part + n_down : -n_small].reshape(F, -1, out_rows, LANES)
            out = [out[:, i].reshape(local_qk, LANES) for i in range(width // LANES)]
            out = jnp.concatenate(out, axis=1)
        small = gathered[:, -n_small:].reshape(F, C, small_pad).astype(wide)
        biases = small[:, :, :own_bias].reshape(-1)
        gains = small[:, :, own_bias : own_bias + 2 * depth].reshape(F * C, 2, depth)
        gains = gains.transpose(1, 0, 2).reshape(2, width)
        shifts = small[:, :, own_bias + 2 * depth : own_small].reshape(F * C, 2, depth)
        shifts = shifts.transpose(1, 0, 2).reshape(2, width)
        b_qkv = biases[: 3 * width].reshape(3, C, local_qk)
        b_qkv = lax.dynamic_slice_in_dim(b_qkv, place, 1, 1).reshape(-1)
        b_up = biases[5 * width :].reshape(F, C, hidden)
        b_up = lax.dynamic_slice_in_dim(b_up, place, 1, 1).reshape(-1)
        b_rest = biases[3 * width : 4 * width] + biases[4 * width : 5 * width]
        return (
            qkv,
            out,
            up,
            down,
            gains,
            shifts,
            b_qkv[None],
            b_up[None],
            b_rest,
        )

    def sum_rows(partial):
        parts = partial.reshape(C, micros * rows, width)
        parts = lax.all_to_all(parts, "ctx", 0, 0, tiled=False)
        return jnp.sum(parts.astype(wide), axis=0)

    def gather_rows(own):
        return lax.all_gather(own, "ctx", axis=0).reshape(total_rows, width)

    positions = jnp.arange(pack_len, dtype=jnp.int32)
    seg = segments_of(doc_lengths[:, 0], positions)
    visible = (positions[None, None, :] <= positions[None, :, None]) & (
        seg[:, None, :] == seg[:, :, None]
    )
    visible = visible.astype(wide)
    row_positions = jnp.broadcast_to(positions.reshape(C, 1, rows), (C, micros, rows))
    tables = rotary_tables(row_positions.reshape(-1), local_qk)
    square = (micros * heads, pack_len, pack_len)
    forward_outs = [
        ((total_rows, width), low),
        ((total_rows, width), low),
        ((total_rows, width), low),
        ((total_rows, 3 * local_qk), low),
        (square, wide),
        ((total_rows, local_qk), low),
        ((total_rows, local_ff), wide),
        ((total_rows, local_ff), low),
    ]
    backward_outs = [
        ((total_rows, width), low),
        ((width, 3 * local_qk), low),
        ((local_qk, width), low),
        ((width, local_ff), low),
        ((local_ff, width), low),
        ((1, 3 * local_qk), wide),
        ((1, local_ff), wide),
        ((2, width), wide),
        ((2, width), wide),
    ]
    backward_scratch = [((total_rows, 3 * local_qk), wide), ((total_rows, 3 * local_qk), low)]

    kept_layers = []
    all_weights = []
    gathered = [gather_layer(layer) for layer in range(layers)]
    own_values = tokens_rows.astype(wide)
    for layer in range(layers):
        if layer > 0:
            gathered[layer], values_all = lax.optimization_barrier((gathered[layer], values_all))
        weights = layer_weights(gathered[layer])
        all_weights.append(weights)
        qkv, out, up, down, gains, shifts, b_qkv, b_up, b_rest = weights
        change, *kept = call(
            functools.partial(forward_kernel, micros, C),
            forward_outs,
            [],
            values_all,
            qkv,
            out,
            up,
            down,
            gains,
            shifts,
            b_qkv,
            b_up,
            tables,
            visible,
        )
        kept_layers.append((values_all, own_values, kept))
        change = sum_rows(change) + b_rest
        if layer + 1 < layers:
            change = change.astype(low)
            values_all = values_all + gather_rows(change).astype(wide)
            change = change.astype(wide)
        own_values = own_values + change
    block_out = own_values.astype(low).reshape(micros, 1, rows, width)

    own_grad = cot_rows.astype(wide)
    cot_low = cot_all
    mine = (jnp.arange(C) == place).astype(wide)
    pieces = [None] * layers
    for layer in reversed(range(layers)):
        qkv, out, up, down, gains, shifts, b_qkv, b_up, b_rest = all_weights[layer]
        values, own_in, kept = kept_layers[layer]
        db_rest = jnp.sum(own_grad.astype(low).astype(wide), axis=0)
        flow, d_qkv, d_out, d_up, d_down, db_qkv, db_up, dg, ds = call(
            functools.partial(backward_kernel, micros, C),
            backward_outs,
            backward_scratch,
            cot_low,
            values,
            qkv,
            out,
            up,
            down,
            gains,
            tables,
            *kept,
        )
        flow = sum_rows(flow)
        unit_own, inverse = normalise(own_in)
        flow = flow - jnp.mean(flow, axis=-1, keepdims=True) - unit_own * jnp.mean(
            flow * unit_own, axis=-1, keepdims=True
        )
        own_grad = own_grad + inverse * flow
        if layer > 0:
            cot_low = gather_rows(own_grad.astype(low))

        db_qkv = (db_qkv.reshape(3, 1, local_qk) * mine[None, :, None]).reshape(-1)
        db_up = (db_up.reshape(F, 1, hidden) * mine[None, :, None]).reshape(-1)
        db = jnp.concatenate([db_qkv, db_rest, db_rest, db_up]).reshape(F * C, own_bias)
        dg = dg.reshape(2, F * C, depth).transpose(1, 0, 2).reshape(F * C, 2 * depth)
        ds = ds.reshape(2, F * C, depth).transpose(1, 0, 2).reshape(F * C, 2 * depth)
        small = jnp.concatenate(
            [db, dg, ds, jnp.zeros((F * C, small_pad - own_small), wide)], axis=1
        )
        small = small.astype(low).reshape(F, -1, LANES)
        extra = -small.shape[1] % 16
        small = jnp.pad(small, ((0, 0), (0, extra), (0, 0)))
        if aligned:
            size = (column_slabs * C * depth) + width // LANES * (hidden + out_rows)
            (payload,) = call(
                pack_kernel,
                [((F, size + small.shape[1], LANES), low)],
                [],
                d_qkv,
                d_up,
                d_down,
                d_out,
                small,
            )
        else:
            payload = jnp.concatenate(
                slabs(d_qkv.reshape(F, C * depth, 3 * local_qk))
                + slabs(d_up.reshape(F, C * depth, local_ff))
                + slabs(d_down.reshape(F, hidden, width))
                + slabs(d_out.reshape(F, out_rows, width))
                + [small],
                axis=1,
            )
        parts = lax.all_to_all(payload, "fsdp", 0, 0, tiled=False)
        pieces[layer] = jnp.sum(parts.astype(wide), axis=0)
        pieces[layer] = pieces[layer][: pieces[layer].shape[0] - extra]
    grad_tokens = own_grad.reshape(micros, 1, rows, width)

    merged = jnp.stack(pieces)
    n_cols = column_slabs * C * depth
    n_down = width // LANES * hidden
    n_out = width // LANES * out_rows
    cols = merged[:, :n_cols].reshape(layers, column_slabs, C, depth, LANES)
    cols = cols.transpose(2, 0, 1, 3, 4).reshape(C, layers, -1, LANES)
    small = merged[:, n_cols + n_down + n_out :].reshape(layers, C, -1, LANES).transpose(1, 0, 2, 3)
    home = lax.all_to_all(jnp.concatenate([cols, small], axis=2), "ctx", 0, 0, tiled=False)
    down_sum = merged[:, n_cols : n_cols + n_down].reshape(layers, -1, hidden, LANES)
    grad_down = down_sum.transpose(0, 2, 1, 3).reshape(layers, hidden, width)
    out_sum = merged[:, n_cols + n_down : n_cols + n_down + n_out]
    out_sum = out_sum.reshape(layers, -1, out_rows, LANES).transpose(0, 2, 1, 3)
    grad_out = lax.ppermute(out_sum.reshape(layers, out_rows, width), ("fsdp", "ctx"), back)

    n_own = column_slabs * depth
    columns = home[:, :, :n_own].reshape(C, layers, column_slabs, depth, LANES)
    grad_qkv = columns[:, :, :3].transpose(1, 3, 2, 0, 4).reshape(layers, depth, 3 * width)
    grad_up = columns[:, :, 3:].transpose(0, 1, 3, 2, 4).reshape(C, layers, depth, F, hidden)
    grad_up = grad_up.transpose(1, 2, 3, 0, 4).reshape(layers, depth, F * C * hidden)
    small = jnp.sum(home[:, :, n_own:], axis=0).reshape(layers, small_pad)
    grad_bias = small[:, :own_bias]
    grad_gain = small[:, own_bias : own_bias + 2 * depth].reshape(layers, 2, depth)
    grad_shift = small[:, own_bias + 2 * depth : own_small].reshape(layers, 2, depth)
    return (
        block_out,
        grad_tokens,
        grad_qkv,
        grad_out,
        grad_up,
        grad_down,
        grad_gain,
        grad_shift,
        grad_bias,
    )


def solution(mesh):
    weight = P(None, ("fsdp", "ctx"), None)
    rows = P(None, "fsdp", "ctx", None)
    feature = P(None, None, ("fsdp", "ctx"))
    flat = P(None, ("fsdp", "ctx"))
    return jax.shard_map(
        body,
        mesh=mesh,
        in_specs=(
            rows,
            rows,
            P(None, "fsdp", None),
            weight,
            weight,
            weight,
            weight,
            feature,
            feature,
            flat,
        ),
        out_specs=(rows, rows, weight, weight, weight, weight, feature, feature, flat),
        check_vma=False,
    )
```
